256 devices in a mesh: dp: 32 (over z_lo, x, core), tensor: 8 (over y, z_hi).
Axes of the slice: x: 4, y: 4, z: 8 (z_hi: 2, z_lo: 4; z = z_hi * 4 + z_lo), core: 2. Of those that a mesh axis runs over, the one named last changes fastest.
Arguments:
- up_inputs: bfloat16 [32, 256, 8192], P('dp', None, 'tensor'), may hold values from -6 to 6
- up_grads: bfloat16 [32, 256, 28672], P('dp', None, 'tensor'), may hold values from -6 to 6
- down_inputs: bfloat16 [32, 256, 28672], P('dp', None, 'tensor'), may hold values from -6 to 6
- down_grads: bfloat16 [32, 256, 8192], P('dp', None, 'tensor'), may hold values from -6 to 6
- up_in_proj: bfloat16 [8192, 64], P('tensor'), may hold values from -0.0625 to 0.0625
- up_out_proj: bfloat16 [28672, 64], P('tensor'), may hold values from -0.03125 to 0.03125
- down_in_proj: bfloat16 [28672, 64], P('tensor'), may hold values from -0.03125 to 0.03125
- down_out_proj: bfloat16 [8192, 64], P('tensor'), may hold values from -0.0625 to 0.0625
- queries: bfloat16 [4096, 8192], P('dp', 'tensor'), may hold values from -0.015625 to 0.015625
Outputs:
- scores: float32 [32, 4096], P(None, 'dp')
The draws below stay inside these ranges and needn't reach their ends.
All inputs are finite; a program needn't handle non-finite values.
Results may differ from the reference program's by a relative error of at most 0.0029.
Values may be sent and summed in bfloat16 or wider, within the bound.
No kernel may reach another device: no remote copies, remote signals or barrier semaphores. Data moves between devices by JAX's collectives and lax.ppermute only.
A program may use at most 64 MiB of HBM per device.

```python
import jax
import jax.numpy as jnp
from jax import lax

D = 8192
FF = 28672
RANK = 64
QUERIES = 4096
SEQ = 256
EXAMPLES = 32


def level_of(rng, shape, pieces, low, high):
    factor_of = 1.0
    for axis_at, parts in pieces:
        steps = jax.random.uniform(jax.random.fold_in(jax.random.fold_in(rng, 6), axis_at), (parts,), jnp.float32, low / len(pieces), high / len(pieces))
        factor_of = factor_of * jnp.repeat(jnp.exp(steps), shape[axis_at] // parts).reshape((-1,) + (1,) * (len(shape) - 1 - axis_at))
    return factor_of


def gaussian(key, shape, deviation, reach, cuts=(), kind=jnp.bfloat16):
    drawn = jax.random.normal(key, shape, jnp.float32) * deviation
    if len(cuts) > 0:
        drawn = level_of(key, shape, cuts, -0.22, 0.18) * drawn
    return jnp.clip(drawn, min=-reach, max=reach).astype(kind)


def setup_inputs(seed: int = 0) -> dict:
    key_list = jax.random.split(jax.random.key(seed), 10)
    up_inputs = gaussian(key_list[0], (EXAMPLES, SEQ, D), 1.0, 6.0, ((0, 32), (2, 8)))
    up_grads = gaussian(key_list[1], (EXAMPLES, SEQ, FF), 1.0, 6.0, ((0, 32), (2, 8)))
    down_inputs = gaussian(key_list[2], (EXAMPLES, SEQ, FF), 1.0, 6.0, ((0, 32), (2, 8)))
    down_grads = gaussian(key_list[3], (EXAMPLES, SEQ, D), 1.0, 6.0, ((0, 32), (2, 8)))
    up_in_proj = gaussian(key_list[4], (D, RANK), D ** -0.5, 0.0625, ((0, 8),))
    up_out_proj = gaussian(key_list[5], (FF, RANK), FF ** -0.5, 0.03125, ((0, 8),))
    down_in_proj = gaussian(key_list[6], (FF, RANK), FF ** -0.5, 0.03125, ((0, 8),))
    down_out_proj = gaussian(key_list[7], (D, RANK), D ** -0.5, 0.0625, ((0, 8),))
    queries = gaussian(key_list[8], (QUERIES, 2 * RANK * RANK), (0.25 / SEQ), 0.015625, ((0, 32), (1, 8)))
    return dict(up_inputs=up_inputs, up_grads=up_grads, down_inputs=down_inputs, down_grads=down_grads, up_in_proj=up_in_proj, up_out_proj=up_out_proj, down_in_proj=down_in_proj, down_out_proj=down_out_proj, queries=queries)


def project_rows(acts, proj):
    ex, seq, wid = acts.shape
    return jnp.dot(acts.reshape(ex * seq, wid), proj, preferred_element_type=jnp.float32).reshape(ex, seq, -1)


def outer_sum(outs, ins):
    summed = jnp.einsum("esr,esc->erc", outs.astype(jnp.float32), ins.astype(jnp.float32), precision=lax.Precision.HIGHEST)
    return summed.reshape(outs.shape[0], -1)


def reference(up_inputs, up_grads, down_inputs, down_grads, up_in_proj, up_out_proj, down_in_proj, down_out_proj, queries):
    up_in = project_rows(up_inputs, up_in_proj)
    up_out = project_rows(up_grads, up_out_proj)
    down_in = project_rows(down_inputs, down_in_proj)
    down_out = project_rows(down_grads, down_out_proj)
    projected = jnp.concatenate([outer_sum(up_out, up_in), outer_sum(down_out, down_in)], axis=1)
    packed = projected.astype(jnp.bfloat16)
    return lax.dot_general(packed, queries, (((1,), (1,)), ((), ())), preferred_element_type=jnp.float32)
```

```python
import jax
import jax.numpy as jnp
from jax import lax
from jax.sharding import Mesh, PartitionSpec as P

SIZES = (4, 4, 2, 4, 2)
NAMES = ("zl", "x", "c", "y", "zh")
DP = ("zl", "x", "c")
TENSOR = ("y", "zh")


def project_columns(acts, proj):
    return lax.dot_general(
        proj, acts[0], (((0,), (1,)), ((), ())), preferred_element_type=jnp.float32
    )


def outer_rows(outs, ins):
    return lax.dot_general(
        outs, ins, (((1,), (1,)), ((), ())),
        precision=lax.Precision.HIGHEST, preferred_element_type=jnp.float32,
    )


def exchange(pieces, axes):
    return lax.all_to_all(pieces, axes, split_axis=0, concat_axis=0, tiled=True)


def swap(values, axis, mask):
    size = lax.axis_size(axis)
    return lax.ppermute(values, axis, [(k, k ^ mask) for k in range(size)])


def to_all(held, axes, size):
    return exchange(jnp.broadcast_to(held, (size,) + held.shape), axes)


def per_device(
    up_inputs,
    up_grads,
    down_inputs,
    down_grads,
    up_in_proj,
    up_out_proj,
    down_in_proj,
    down_out_proj,
    queries,
):
    zls, xs, cores, ys, zhs = SIZES
    rank = up_in_proj.shape[1]
    rows = 2 * rank // ys // zhs
    other = swap(queries, "zh", 1)
    up_in = project_columns(up_inputs, up_in_proj)
    down_out = project_columns(down_grads, down_out_proj)
    wide_proj = jnp.concatenate([up_out_proj, down_in_proj], axis=1)
    wide_proj, up_in, down_out = lax.optimization_barrier((wide_proj, up_in, down_out))
    up_out = project_columns(up_grads, wide_proj[:, :rank])
    down_in = project_columns(down_inputs, wide_proj[:, rank:])
    pieces = []
    for outs, ins in ((up_out, up_in), (down_out, down_in)):
        for k in range(rank // (zhs * rows)):
            pieces.append(jnp.concatenate([outs[k * zhs * rows : (k + 1) * zhs * rows], ins], axis=0))
    pieces = jnp.stack(pieces)
    y = lax.axis_index("y")
    piece = lambda k: lax.dynamic_index_in_dim(pieces, k, 0, keepdims=False)
    half = piece(y) + sum(swap(piece(y ^ mask), "y", mask) for mask in (1, 3, 2))
    sums = half + swap(half, "zh", 1)
    outer = zhs * rows
    outs, ins = sums[:outer], sums[outer:]
    own = jnp.concatenate([outer_rows(outs[0::2], ins), outer_rows(outs[1::2], ins)], axis=1)
    every = to_all(own.astype(jnp.bfloat16), DP, zls * xs * cores)
    first_half = lax.axis_index("zh") == 0
    low, high = jnp.where(first_half, queries, other), jnp.where(first_half, other, queries)
    scores = lax.dot_general(
        every.reshape(every.shape[0], -1), jnp.concatenate([low, high], axis=1), (((1,), (1,)), ((), ())),
        preferred_element_type=jnp.float32,
    )
    from_1, from_2, from_3 = (swap(scores, "y", mask) for mask in (1, 2, 3))
    return (from_2 + from_3) + (from_1 + scores)


def solution(mesh):
    split = Mesh(mesh.devices.reshape(SIZES), NAMES)
    placed = (
        P(DP, None, TENSOR),
        P(DP, None, TENSOR),
        P(DP, None, TENSOR),
        P(DP, None, TENSOR),
        P(TENSOR, None),
        P(TENSOR, None),
        P(TENSOR, None),
        P(TENSOR, None),
        P(DP, TENSOR),
    )
    return jax.shard_map(
        per_device, mesh=split, in_specs=placed, out_specs=P(None, DP), check_vma=False
    )
```

```python
import jax
import jax.numpy as jnp
from jax import lax
from jax.sharding import Mesh, PartitionSpec as P

SIZES = (4, 4, 2, 4, 2)
NAMES = ("zl", "x", "c", "y", "zh")
DP = ("zl", "x", "c")
TENSOR = ("y", "zh")


def project_columns(acts, proj):
    return lax.dot_general(
        proj, acts[0], (((0,), (1,)), ((), ())), preferred_element_type=jnp.float32
    )


def rounded(values):
    return lax.reduce_precision(values, 8, 7)


def in_16_bits(sums, outer):
    high = rounded(sums[:outer])
    return jnp.concatenate([high, rounded(sums[:outer] - high), rounded(sums[outer:])], axis=0)


def sum_of_parts(parts, outer):
    return parts[:outer] + parts[outer : 2 * outer], parts[2 * outer :]


def outer_rows(outs, ins):
    return lax.dot_general(
        outs, ins, (((1,), (1,)), ((), ())),
        precision=lax.Precision.HIGHEST, preferred_element_type=jnp.float32,
    )


def exchange(pieces, axes):
    return lax.all_to_all(pieces, axes, split_axis=0, concat_axis=0, tiled=True)


def swap(values, axis, mask):
    size = lax.axis_size(axis)
    return lax.ppermute(values, axis, [(k, k ^ mask) for k in range(size)])


def to_all(held, axes, size):
    return exchange(jnp.broadcast_to(held, (size,) + held.shape), axes)


def per_device(
    up_inputs,
    up_grads,
    down_inputs,
    down_grads,
    up_in_proj,
    up_out_proj,
    down_in_proj,
    down_out_proj,
    queries,
):
    zls, xs, cores, ys, zhs = SIZES
    rank = up_in_proj.shape[1]
    rows = 2 * rank // ys // zhs
    other = swap(queries, "zh", 1)
    up_in = project_columns(up_inputs, up_in_proj)
    down_out = project_columns(down_grads, down_out_proj)
    wide_proj = jnp.concatenate([up_out_proj, down_in_proj], axis=1)
    wide_proj, up_in, down_out = lax.optimization_barrier((wide_proj, up_in, down_out))
    up_out = project_columns(up_grads, wide_proj[:, :rank])
    down_in = project_columns(down_inputs, wide_proj[:, rank:])
    pieces = []
    for outs, ins in ((up_out, up_in), (down_out, down_in)):
        for k in range(rank // (zhs * rows)):
            pieces.append(jnp.concatenate([outs[k * zhs * rows : (k + 1) * zhs * rows], ins], axis=0))
    pieces = jnp.stack(pieces)
    y = lax.axis_index("y")
    piece = lambda k: lax.dynamic_index_in_dim(pieces, k, 0, keepdims=False)
    half = piece(y) + sum(swap(piece(y ^ mask), "y", mask) for mask in (1, 3, 2))
    outer = zhs * rows
    parts = in_16_bits(half, outer)
    near = sum_of_parts(parts, outer)
    far = sum_of_parts(swap(parts.astype(jnp.bfloat16), "zh", 1).astype(jnp.float32), outer)
    outs, ins = near[0] + far[0], near[1] + far[1]
    own = jnp.concatenate([outer_rows(outs[0::2], ins), outer_rows(outs[1::2], ins)], axis=1)
    every = to_all(own.astype(jnp.bfloat16), DP, zls * xs * cores)
    first_half = lax.axis_index("zh") == 0
    low, high = jnp.where(first_half, queries, other), jnp.where(first_half, other, queries)
    scores = lax.dot_general(
        every.reshape(every.shape[0], -1), jnp.concatenate([low, high], axis=1), (((1,), (1,)), ((), ())),
        preferred_element_type=jnp.float32,
    )
    from_1, from_2, from_3 = (swap(scores, "y", mask) for mask in (1, 2, 3))
    return (from_2 + from_3) + (from_1 + scores)


def solution(mesh):
    split = Mesh(mesh.devices.reshape(SIZES), NAMES)
    placed = (
        P(DP, None, TENSOR),
        P(DP, None, TENSOR),
        P(DP, None, TENSOR),
        P(DP, None, TENSOR),
        P(TENSOR, None),
        P(TENSOR, None),
        P(TENSOR, None),
        P(TENSOR, None),
        P(DP, TENSOR),
    )
    return jax.shard_map(
        per_device, mesh=split, in_specs=placed, out_specs=P(None, DP), check_vma=False
    )
```

```python
import jax
import jax.numpy as jnp
from jax import lax
from jax.sharding import Mesh, PartitionSpec as P

SIZES = (4, 4, 2, 4, 2)
NAMES = ("zl", "x", "c", "y", "zh")
DP = ("zl", "x", "c")
TENSOR = ("y", "zh")


def project_columns(acts, proj):
    return lax.dot_general(
        proj, acts[0], (((0,), (1,)), ((), ())), preferred_element_type=jnp.float32
    )


def outer_rows(outs, ins):
    return lax.dot_general(
        outs, ins, (((1,), (1,)), ((), ())),
        precision=lax.Precision.HIGHEST, preferred_element_type=jnp.float32,
    )


def exchange(pieces, axes):
    return lax.all_to_all(pieces, axes, split_axis=0, concat_axis=0, tiled=True)


def swap(values, axis, mask):
    size = lax.axis_size(axis)
    return lax.ppermute(values, axis, [(k, k ^ mask) for k in range(size)])


def swap_by_core(values, masks):
    ys = lax.axis_size("y")
    pairs = [(c * ys + y, c * ys + (y ^ mask)) for c, mask in enumerate(masks) for y in range(ys)]
    return lax.ppermute(values, ("c", "y"), pairs)


def to_all(held, axes, size):
    return exchange(jnp.broadcast_to(held, (size,) + held.shape), axes)


def per_device(
    up_inputs,
    up_grads,
    down_inputs,
    down_grads,
    up_in_proj,
    up_out_proj,
    down_in_proj,
    down_out_proj,
    queries,
):
    zls, xs, cores, ys, zhs = SIZES
    rank = up_in_proj.shape[1]
    rows = 2 * rank // ys // zhs
    other = swap(queries, "zh", 1)
    up_in = project_columns(up_inputs, up_in_proj)
    down_out = project_columns(down_grads, down_out_proj)
    wide_proj = jnp.concatenate([up_out_proj, down_in_proj], axis=1)
    wide_proj, up_in, down_out = lax.optimization_barrier((wide_proj, up_in, down_out))
    up_out = project_columns(up_grads, wide_proj[:, :rank])
    down_in = project_columns(down_inputs, wide_proj[:, rank:])
    pieces = []
    for outs, ins in ((up_out, up_in), (down_out, down_in)):
        for k in range(rank // (zhs * rows)):
            pieces.append(jnp.concatenate([outs[k * zhs * rows : (k + 1) * zhs * rows], ins], axis=0))
    pieces = jnp.stack(pieces)
    y = lax.axis_index("y")
    piece = lambda k: lax.dynamic_index_in_dim(pieces, k, 0, keepdims=False)
    turns = ((2, 2), (3, 1), (1, 3))
    half = piece(y)
    for masks in turns:
        half = half + swap_by_core(piece(y ^ jnp.where(lax.axis_index("c") == 0, *masks)), masks)
    sums = half + swap(half, "zh", 1)
    outer = zhs * rows
    outs, ins = sums[:outer], sums[outer:]
    own = jnp.concatenate([outer_rows(outs[0::2], ins), outer_rows(outs[1::2], ins)], axis=1)
    every = to_all(own.astype(jnp.bfloat16), DP, zls * xs * cores)
    other, every = lax.optimization_barrier((other, every))
    first_half = lax.axis_index("zh") == 0
    low, high = jnp.where(first_half, queries, other), jnp.where(first_half, other, queries)
    scores = lax.dot_general(
        every.reshape(every.shape[0], -1), jnp.concatenate([low, high], axis=1), (((1,), (1,)), ((), ())),
        preferred_element_type=jnp.float32,
    )
    from_1, from_2, from_3 = (swap(scores, "y", mask) for mask in (1, 2, 3))
    return (from_2 + from_3) + (from_1 + scores)


def solution(mesh):
    split = Mesh(mesh.devices.reshape(SIZES), NAMES)
    placed = (
        P(DP, None, TENSOR),
        P(DP, None, TENSOR),
        P(DP, None, TENSOR),
        P(DP, None, TENSOR),
        P(TENSOR, None),
        P(TENSOR, None),
        P(TENSOR, None),
        P(TENSOR, None),
        P(DP, TENSOR),
    )
    return jax.shard_map(
        per_device, mesh=split, in_specs=placed, out_specs=P(None, DP), check_vma=False
    )
```

```python
import jax
import jax.numpy as jnp
from jax import lax
from jax.sharding import Mesh, PartitionSpec as P

SIZES = (4, 4, 2, 4, 2)
NAMES = ("zl", "x", "c", "y", "zh")
DP = ("zl", "x", "c")
TENSOR = ("y", "zh")


def project_columns(acts, proj):
    return lax.dot_general(
        proj, acts[0], (((0,), (1,)), ((), ())), preferred_element_type=jnp.float32
    )


def outer_rows(outs, ins):
    return lax.dot_general(
        outs, ins, (((1,), (1,)), ((), ())),
        precision=lax.Precision.HIGHEST, preferred_element_type=jnp.float32,
    )


def exchange(pieces, axes):
    return lax.all_to_all(pieces, axes, split_axis=0, concat_axis=0, tiled=True)


def swap(values, axis, mask):
    size = lax.axis_size(axis)
    return lax.ppermute(values, axis, [(k, k ^ mask) for k in range(size)])


def to_all(held, axes, size):
    return exchange(jnp.broadcast_to(held, (size,) + held.shape), axes)


def per_device(
    up_inputs,
    up_grads,
    down_inputs,
    down_grads,
    up_in_proj,
    up_out_proj,
    down_in_proj,
    down_out_proj,
    queries,
):
    zls, xs, _, ys, zhs = SIZES
    rank = up_in_proj.shape[1]
    rows = 2 * rank // ys // zhs
    other = swap(queries, "zh", 1)
    up_in = project_columns(up_inputs, up_in_proj)
    down_out = project_columns(down_grads, down_out_proj)
    wide_proj = jnp.concatenate([up_out_proj, down_in_proj], axis=1)
    wide_proj, up_in, down_out = lax.optimization_barrier((wide_proj, up_in, down_out))
    up_out = project_columns(up_grads, wide_proj[:, :rank])
    down_in = project_columns(down_inputs, wide_proj[:, rank:])
    pieces = []
    for outs, ins in ((up_out, up_in), (down_out, down_in)):
        for k in range(rank // (zhs * rows)):
            pieces.append(jnp.concatenate([outs[k * zhs * rows : (k + 1) * zhs * rows], ins], axis=0))
    pieces = jnp.stack(pieces)
    y = lax.axis_index("y")
    piece = lambda k: lax.dynamic_index_in_dim(pieces, k, 0, keepdims=False)
    half = piece(y) + sum(swap(piece(y ^ mask), "y", mask) for mask in (1, 3, 2))
    sums = half + swap(half, "zh", 1)
    outer = zhs * rows
    outs, ins = sums[:outer], sums[outer:]
    own = jnp.concatenate([outer_rows(outs[0::2], ins), outer_rows(outs[1::2], ins)], axis=1)
    near = to_all(own.astype(jnp.bfloat16), ("zl", "x"), zls * xs)
    far = swap(near, "c", 1)
    second = lax.axis_index("c") == 1
    every = jnp.stack([jnp.where(second, far, near), jnp.where(second, near, far)], axis=1)
    every = every.reshape((-1,) + own.shape)
    first_half = lax.axis_index("zh") == 0
    low, high = jnp.where(first_half, queries, other), jnp.where(first_half, other, queries)
    scores = lax.dot_general(
        every.reshape(every.shape[0], -1), jnp.concatenate([low, high], axis=1), (((1,), (1,)), ((), ())),
        preferred_element_type=jnp.float32,
    )
    from_1, from_2, from_3 = (swap(scores, "y", mask) for mask in (1, 2, 3))
    return (from_2 + from_3) + (from_1 + scores)


def solution(mesh):
    split = Mesh(mesh.devices.reshape(SIZES), NAMES)
    placed = (
        P(DP, None, TENSOR),
        P(DP, None, TENSOR),
        P(DP, None, TENSOR),
        P(DP, None, TENSOR),
        P(TENSOR, None),
        P(TENSOR, None),
        P(TENSOR, None),
        P(TENSOR, None),
        P(DP, TENSOR),
    )
    return jax.shard_map(
        per_device, mesh=split, in_specs=placed, out_specs=P(None, DP), check_vma=False
    )
```

```python
import jax
import jax.numpy as jnp
from jax import lax
from jax.sharding import Mesh, PartitionSpec as P

SIZES = (4, 4, 2, 4, 2)
NAMES = ("zl", "x", "c", "y", "zh")
DP = ("zl", "x", "c")
TENSOR = ("y", "zh")


def project_columns(acts, proj):
    return lax.dot_general(
        proj, acts[0], (((0,), (1,)), ((), ())), preferred_element_type=jnp.float32
    )


def outer_rows(outs, ins):
    return lax.dot_general(
        outs, ins, (((1,), (1,)), ((), ())),
        precision=lax.Precision.HIGHEST, preferred_element_type=jnp.float32,
    )


def exchange(pieces, axes):
    return lax.all_to_all(pieces, axes, split_axis=0, concat_axis=0, tiled=True)


def swap(values, axis, mask):
    size = lax.axis_size(axis)
    return lax.ppermute(values, axis, [(k, k ^ mask) for k in range(size)])


def to_all(held, axes, size):
    return exchange(jnp.broadcast_to(held, (size,) + held.shape), axes)


def per_device(
    up_inputs,
    up_grads,
    down_inputs,
    down_grads,
    up_in_proj,
    up_out_proj,
    down_in_proj,
    down_out_proj,
    queries,
):
    zls, xs, cores, ys, zhs = SIZES
    rank = up_in_proj.shape[1]
    rows = 2 * rank // ys // zhs
    part = queries.shape[0] // 2
    early, late = swap(queries[:part], "zh", 1), swap(queries[part:], "zh", 1)
    up_in = project_columns(up_inputs, up_in_proj)
    down_out = project_columns(down_grads, down_out_proj)
    wide_proj = jnp.concatenate([up_out_proj, down_in_proj], axis=1)
    wide_proj, up_in, down_out = lax.optimization_barrier((wide_proj, up_in, down_out))
    up_out = project_columns(up_grads, wide_proj[:, :rank])
    down_in = project_columns(down_inputs, wide_proj[:, rank:])
    pieces = []
    for outs, ins in ((up_out, up_in), (down_out, down_in)):
        for k in range(rank // (zhs * rows)):
            pieces.append(jnp.concatenate([outs[k * zhs * rows : (k + 1) * zhs * rows], ins], axis=0))
    pieces = jnp.stack(pieces)
    y = lax.axis_index("y")
    piece = lambda k: lax.dynamic_index_in_dim(pieces, k, 0, keepdims=False)
    half = piece(y) + sum(swap(piece(y ^ mask), "y", mask) for mask in (1, 3, 2))
    sums = half + swap(half, "zh", 1)
    sums, early = lax.optimization_barrier((sums, early))
    other = jnp.concatenate([early, late], axis=0)
    outer = zhs * rows
    outs, ins = sums[:outer], sums[outer:]
    own = jnp.concatenate([outer_rows(outs[0::2], ins), outer_rows(outs[1::2], ins)], axis=1)
    every = to_all(own.astype(jnp.bfloat16), DP, zls * xs * cores)
    first_half = lax.axis_index("zh") == 0
    low, high = jnp.where(first_half, queries, other), jnp.where(first_half, other, queries)
    scores = lax.dot_general(
        every.reshape(every.shape[0], -1), jnp.concatenate([low, high], axis=1), (((1,), (1,)), ((), ())),
        preferred_element_type=jnp.float32,
    )
    from_1, from_2, from_3 = (swap(scores, "y", mask) for mask in (1, 2, 3))
    return (from_2 + from_3) + (from_1 + scores)


def solution(mesh):
    split = Mesh(mesh.devices.reshape(SIZES), NAMES)
    placed = (
        P(DP, None, TENSOR),
        P(DP, None, TENSOR),
        P(DP, None, TENSOR),
        P(DP, None, TENSOR),
        P(TENSOR, None),
        P(TENSOR, None),
        P(TENSOR, None),
        P(TENSOR, None),
        P(DP, TENSOR),
    )
    return jax.shard_map(
        per_device, mesh=split, in_specs=placed, out_specs=P(None, DP), check_vma=False
    )
```

```python
import jax
import jax.numpy as jnp
from jax import lax
from jax.sharding import Mesh, PartitionSpec as P

SIZES = (4, 4, 2, 4, 2)
NAMES = ("zl", "x", "c", "y", "zh")
DP = ("zl", "x", "c")
TENSOR = ("y", "zh")


def project_columns(acts, proj):
    return lax.dot_general(
        proj, acts[0], (((0,), (1,)), ((), ())), preferred_element_type=jnp.float32
    )


def to_send(sums, outer):
    high = lax.reduce_precision(sums[:outer], 8, 7)
    return jnp.concatenate([high, sums[:outer] - high, sums[outer:]], axis=0).astype(jnp.bfloat16)


def from_sent(sent, outer):
    sums = sent.astype(jnp.float32)
    return jnp.concatenate([sums[:outer] + sums[outer : 2 * outer], sums[2 * outer :]], axis=0)


def outer_rows(outs, ins):
    return lax.dot_general(
        outs, ins, (((1,), (1,)), ((), ())),
        precision=lax.Precision.HIGHEST, preferred_element_type=jnp.float32,
    )


def exchange(pieces, axes):
    return lax.all_to_all(pieces, axes, split_axis=0, concat_axis=0, tiled=True)


def swap(values, axis, mask):
    size = lax.axis_size(axis)
    return lax.ppermute(values, axis, [(k, k ^ mask) for k in range(size)])


def to_all(held, axes, size):
    return exchange(jnp.broadcast_to(held, (size,) + held.shape), axes)


def per_device(
    up_inputs,
    up_grads,
    down_inputs,
    down_grads,
    up_in_proj,
    up_out_proj,
    down_in_proj,
    down_out_proj,
    queries,
):
    zls, xs, cores, ys, zhs = SIZES
    rank = up_in_proj.shape[1]
    rows = 2 * rank // ys // zhs
    other = swap(queries, "zh", 1)
    wide_proj = lax.optimization_barrier(jnp.concatenate([up_out_proj, down_in_proj], axis=1))
    up_in = project_columns(up_inputs, up_in_proj)
    up_out = project_columns(up_grads, wide_proj[:, :rank])
    down_in = project_columns(down_inputs, wide_proj[:, rank:])
    down_out = project_columns(down_grads, down_out_proj)
    pieces = []
    for outs, ins in ((up_out, up_in), (down_out, down_in)):
        for k in range(rank // (zhs * rows)):
            pieces.append(jnp.concatenate([outs[k * zhs * rows : (k + 1) * zhs * rows], ins], axis=0))
    pieces = jnp.stack(pieces)
    y = lax.axis_index("y")
    piece = lambda k: lax.dynamic_index_in_dim(pieces, k, 0, keepdims=False)
    outer = zhs * rows
    half = piece(y) + sum(
        from_sent(swap(to_send(piece(y ^ mask), outer), "y", mask), outer) for mask in (1, 3, 2)
    )
    sums = half + swap(half, "zh", 1)
    outs, ins = sums[:outer], sums[outer:]
    own = jnp.concatenate([outer_rows(outs[0::2], ins), outer_rows(outs[1::2], ins)], axis=1)
    every = to_all(own.astype(jnp.bfloat16), DP, zls * xs * cores)
    first_half = lax.axis_index("zh") == 0
    low, high = jnp.where(first_half, queries, other), jnp.where(first_half, other, queries)
    scores = lax.dot_general(
        every.reshape(every.shape[0], -1), jnp.concatenate([low, high], axis=1), (((1,), (1,)), ((), ())),
        preferred_element_type=jnp.float32,
    )
    from_1, from_2, from_3 = (swap(scores, "y", mask) for mask in (1, 2, 3))
    return (from_2 + from_3) + (from_1 + scores)


def solution(mesh):
    split = Mesh(mesh.devices.reshape(SIZES), NAMES)
    placed = (
        P(DP, None, TENSOR),
        P(DP, None, TENSOR),
        P(DP, None, TENSOR),
        P(DP, None, TENSOR),
        P(TENSOR, None),
        P(TENSOR, None),
        P(TENSOR, None),
        P(TENSOR, None),
        P(DP, TENSOR),
    )
    return jax.shard_map(
        per_device, mesh=split, in_specs=placed, out_specs=P(None, DP), check_vma=False
    )
```

```python
import jax
import jax.numpy as jnp
from jax import lax
from jax.sharding import Mesh, PartitionSpec as P

SIZES = (4, 4, 2, 4, 2)
NAMES = ("zl", "x", "c", "y", "zh")
DP = ("zl", "x", "c")
TENSOR = ("y", "zh")


def project_columns(acts, proj):
    return lax.dot_general(
        proj, acts[0], (((0,), (1,)), ((), ())), preferred_element_type=jnp.float32
    )


def to_send(sums, outer):
    high = lax.reduce_precision(sums[:outer], 8, 7)
    return jnp.concatenate([high, sums[:outer] - high, sums[outer:]], axis=0).astype(jnp.bfloat16)


def from_sent(sent, outer):
    sums = sent.astype(jnp.float32)
    return jnp.concatenate([sums[:outer] + sums[outer : 2 * outer], sums[2 * outer :]], axis=0)


def outer_rows(outs, ins):
    return lax.dot_general(
        outs, ins, (((1,), (1,)), ((), ())),
        precision=lax.Precision.HIGHEST, preferred_element_type=jnp.float32,
    )


def exchange(pieces, axes):
    return lax.all_to_all(pieces, axes, split_axis=0, concat_axis=0, tiled=True)


def swap(values, axis, mask):
    size = lax.axis_size(axis)
    return lax.ppermute(values, axis, [(k, k ^ mask) for k in range(size)])


def to_all(held, axes, size):
    return exchange(jnp.broadcast_to(held, (size,) + held.shape), axes)


def per_device(
    up_inputs,
    up_grads,
    down_inputs,
    down_grads,
    up_in_proj,
    up_out_proj,
    down_in_proj,
    down_out_proj,
    queries,
):
    zls, xs, cores, ys, zhs = SIZES
    rank = up_in_proj.shape[1]
    rows = 2 * rank // ys // zhs
    other = swap(queries, "zh", 1)
    up_in = project_columns(up_inputs, up_in_proj)
    wide_proj = jnp.concatenate([up_out_proj, down_in_proj], axis=1)
    wide_proj, up_in = lax.optimization_barrier((wide_proj, up_in))
    up_out = project_columns(up_grads, wide_proj[:, :rank])
    down_in = project_columns(down_inputs, wide_proj[:, rank:])
    down_out = project_columns(down_grads, down_out_proj)
    pieces = []
    for outs, ins in ((up_out, up_in), (down_out, down_in)):
        for k in range(rank // (zhs * rows)):
            pieces.append(jnp.concatenate([outs[k * zhs * rows : (k + 1) * zhs * rows], ins], axis=0))
    pieces = jnp.stack(pieces)
    y = lax.axis_index("y")
    piece = lambda k: lax.dynamic_index_in_dim(pieces, k, 0, keepdims=False)
    outer = zhs * rows
    half = piece(y) + sum(
        from_sent(swap(to_send(piece(y ^ mask), outer), "y", mask), outer) for mask in (1, 3, 2)
    )
    sums = half + swap(half, "zh", 1)
    outs, ins = sums[:outer], sums[outer:]
    own = jnp.concatenate([outer_rows(outs[0::2], ins), outer_rows(outs[1::2], ins)], axis=1)
    every = to_all(own.astype(jnp.bfloat16), DP, zls * xs * cores)
    first_half = lax.axis_index("zh") == 0
    low, high = jnp.where(first_half, queries, other), jnp.where(first_half, other, queries)
    scores = lax.dot_general(
        every.reshape(every.shape[0], -1), jnp.concatenate([low, high], axis=1), (((1,), (1,)), ((), ())),
        preferred_element_type=jnp.float32,
    )
    from_1, from_2, from_3 = (swap(scores, "y", mask) for mask in (1, 2, 3))
    return (from_2 + from_3) + (from_1 + scores)


def solution(mesh):
    split = Mesh(mesh.devices.reshape(SIZES), NAMES)
    placed = (
        P(DP, None, TENSOR),
        P(DP, None, TENSOR),
        P(DP, None, TENSOR),
        P(DP, None, TENSOR),
        P(TENSOR, None),
        P(TENSOR, None),
        P(TENSOR, None),
        P(TENSOR, None),
        P(DP, TENSOR),
    )
    return jax.shard_map(
        per_device, mesh=split, in_specs=placed, out_specs=P(None, DP), check_vma=False
    )
```

```python
import jax
import jax.numpy as jnp
from jax import lax
from jax.sharding import Mesh, PartitionSpec as P

SIZES = (4, 4, 2, 4, 2)
NAMES = ("zl", "x", "c", "y", "zh")
DP = ("zl", "x", "c")
TENSOR = ("y", "zh")


def project_columns(acts, proj):
    return lax.dot_general(
        proj, acts[0], (((0,), (1,)), ((), ())), preferred_element_type=jnp.float32
    )


def to_send(sums, outer):
    high = lax.reduce_precision(sums[:outer], 8, 7)
    return jnp.concatenate([high, sums[:outer] - high, sums[outer:]], axis=0).astype(jnp.bfloat16)


def from_sent(sent, outer):
    sums = sent.astype(jnp.float32)
    return jnp.concatenate([sums[:outer] + sums[outer : 2 * outer], sums[2 * outer :]], axis=0)


def outer_rows(outs, ins):
    return lax.dot_general(
        outs, ins, (((1,), (1,)), ((), ())),
        precision=lax.Precision.HIGHEST, preferred_element_type=jnp.float32,
    )


def exchange(pieces, axes):
    return lax.all_to_all(pieces, axes, split_axis=0, concat_axis=0, tiled=True)


def swap(values, axis, mask):
    size = lax.axis_size(axis)
    return lax.ppermute(values, axis, [(k, k ^ mask) for k in range(size)])


def to_all(held, axes, size):
    return exchange(jnp.broadcast_to(held, (size,) + held.shape), axes)


def per_device(
    up_inputs,
    up_grads,
    down_inputs,
    down_grads,
    up_in_proj,
    up_out_proj,
    down_in_proj,
    down_out_proj,
    queries,
):
    zls, xs, cores, ys, zhs = SIZES
    rank = up_in_proj.shape[1]
    rows = 2 * rank // ys // zhs
    other = swap(queries, "zh", 1)
    wide_proj = lax.optimization_barrier(jnp.concatenate([up_out_proj, down_in_proj], axis=1))
    up_in = project_columns(up_inputs, up_in_proj)
    up_out = project_columns(up_grads, wide_proj[:, :rank])
    down_in = project_columns(down_inputs, wide_proj[:, rank:])
    down_out = project_columns(down_grads, down_out_proj)
    pieces = []
    for outs, ins in ((up_out, up_in), (down_out, down_in)):
        for k in range(rank // (zhs * rows)):
            pieces.append(jnp.concatenate([outs[k * zhs * rows : (k + 1) * zhs * rows], ins], axis=0))
    pieces = jnp.stack(pieces)
    y = lax.axis_index("y")
    piece = lambda k: lax.dynamic_index_in_dim(pieces, k, 0, keepdims=False)
    outer = zhs * rows
    half = piece(y) + sum(
        from_sent(swap(to_send(piece(y ^ mask), outer), "y", mask), outer) for mask in (1, 3, 2)
    )
    sums = half + swap(half, "zh", 1)
    outs, ins = sums[:outer], sums[outer:]
    own = jnp.concatenate([outer_rows(outs[0::2], ins), outer_rows(outs[1::2], ins)], axis=1)
    every = to_all(own.astype(jnp.bfloat16), DP[::-1], zls * xs * cores)
    every = every.reshape((cores, xs, zls) + own.shape).transpose(2, 1, 0, 3, 4).reshape(every.shape)
    first_half = lax.axis_index("zh") == 0
    low, high = jnp.where(first_half, queries, other), jnp.where(first_half, other, queries)
    scores = lax.dot_general(
        every.reshape(every.shape[0], -1), jnp.concatenate([low, high], axis=1), (((1,), (1,)), ((), ())),
        preferred_element_type=jnp.float32,
    )
    from_1, from_2, from_3 = (swap(scores, "y", mask) for mask in (1, 2, 3))
    return (from_2 + from_3) + (from_1 + scores)


def solution(mesh):
    split = Mesh(mesh.devices.reshape(SIZES), NAMES)
    placed = (
        P(DP, None, TENSOR),
        P(DP, None, TENSOR),
        P(DP, None, TENSOR),
        P(DP, None, TENSOR),
        P(TENSOR, None),
        P(TENSOR, None),
        P(TENSOR, None),
        P(TENSOR, None),
        P(DP, TENSOR),
    )
    return jax.shard_map(
        per_device, mesh=split, in_specs=placed, out_specs=P(None, DP), check_vma=False
    )
```

```python
import jax
import jax.numpy as jnp
from jax import lax
from jax.sharding import Mesh, PartitionSpec as P

SIZES = (4, 4, 2, 4, 2)
NAMES = ("zl", "x", "c", "y", "zh")
DP = ("zl", "x", "c")
TENSOR = ("y", "zh")


def project_columns(acts, proj):
    return lax.dot_general(
        proj, acts[0], (((0,), (1,)), ((), ())), preferred_element_type=jnp.float32
    )


def to_send(sums, outer):
    high = lax.reduce_precision(sums[:outer], 8, 7)
    return jnp.concatenate([high, sums[:outer] - high, sums[outer:]], axis=0).astype(jnp.bfloat16)


def from_sent(sent, outer):
    sums = sent.astype(jnp.float32)
    return jnp.concatenate([sums[:outer] + sums[outer : 2 * outer], sums[2 * outer :]], axis=0)


def outer_rows(outs, ins):
    return lax.dot_general(
        outs, ins, (((1,), (1,)), ((), ())),
        precision=lax.Precision.HIGHEST, preferred_element_type=jnp.float32,
    )


def exchange(pieces, axes):
    return lax.all_to_all(pieces, axes, split_axis=0, concat_axis=0, tiled=True)


def swap(values, axis, mask):
    size = lax.axis_size(axis)
    return lax.ppermute(values, axis, [(k, k ^ mask) for k in range(size)])


def to_all(held, axes, size):
    return exchange(jnp.broadcast_to(held, (size,) + held.shape), axes)


def per_device(
    up_inputs,
    up_grads,
    down_inputs,
    down_grads,
    up_in_proj,
    up_out_proj,
    down_in_proj,
    down_out_proj,
    queries,
):
    zls, xs, cores, ys, zhs = SIZES
    rank = up_in_proj.shape[1]
    rows = 2 * rank // ys // zhs
    other = swap(queries, "zh", 1)
    wide_proj = lax.optimization_barrier(jnp.concatenate([up_out_proj, down_in_proj], axis=1))
    up_in = project_columns(up_inputs, up_in_proj)
    up_out = project_columns(up_grads, wide_proj[:, :rank])
    down_in = project_columns(down_inputs, wide_proj[:, rank:])
    down_out = project_columns(down_grads, down_out_proj)
    pieces = []
    for outs, ins in ((up_out, up_in), (down_out, down_in)):
        for k in range(rank // (zhs * rows)):
            pieces.append(jnp.concatenate([outs[k * zhs * rows : (k + 1) * zhs * rows], ins], axis=0))
    pieces = jnp.stack(pieces)
    y = lax.axis_index("y")
    piece = lambda k: lax.dynamic_index_in_dim(pieces, k, 0, keepdims=False)
    outer = zhs * rows
    half = piece(y) + sum(
        from_sent(swap(to_send(piece(y ^ mask), outer), "y", mask), outer) for mask in (1, 3, 2)
    )
    sums = half + swap(half, "zh", 1)
    outs, ins = sums[:outer], sums[outer:]
    own = outer_rows(jnp.concatenate([outs[0::2], outs[1::2]], axis=0), ins)
    own = jnp.concatenate([own[:rows], own[rows:]], axis=1)
    every = to_all(own.astype(jnp.bfloat16), DP, zls * xs * cores)
    first_half = lax.axis_index("zh") == 0
    low, high = jnp.where(first_half, queries, other), jnp.where(first_half, other, queries)
    scores = lax.dot_general(
        every.reshape(every.shape[0], -1), jnp.concatenate([low, high], axis=1), (((1,), (1,)), ((), ())),
        preferred_element_type=jnp.float32,
    )
    from_1, from_2, from_3 = (swap(scores, "y", mask) for mask in (1, 2, 3))
    return (from_2 + from_3) + (from_1 + scores)


def solution(mesh):
    split = Mesh(mesh.devices.reshape(SIZES), NAMES)
    placed = (
        P(DP, None, TENSOR),
        P(DP, None, TENSOR),
        P(DP, None, TENSOR),
        P(DP, None, TENSOR),
        P(TENSOR, None),
        P(TENSOR, None),
        P(TENSOR, None),
        P(TENSOR, None),
        P(DP, TENSOR),
    )
    return jax.shard_map(
        per_device, mesh=split, in_specs=placed, out_specs=P(None, DP), check_vma=False
    )
```

```python
import jax
import jax.numpy as jnp
from jax import lax
from jax.sharding import Mesh, PartitionSpec as P

SIZES = (4, 4, 2, 4, 2)
NAMES = ("zl", "x", "c", "y", "zh")
DP = ("zl", "x", "c")
TENSOR = ("y", "zh")


def project_columns(acts, proj):
    return lax.dot_general(
        proj, acts[0], (((0,), (1,)), ((), ())), preferred_element_type=jnp.float32
    )


def to_send(sums, outer):
    high = lax.reduce_precision(sums[:outer], 8, 7)
    return jnp.concatenate([high, sums[:outer] - high, sums[outer:]], axis=0).astype(jnp.bfloat16)


def from_sent(sent, outer):
    sums = sent.astype(jnp.float32)
    return jnp.concatenate([sums[:outer] + sums[outer : 2 * outer], sums[2 * outer :]], axis=0)


def outer_rows(outs, ins):
    return lax.dot_general(
        outs, ins, (((1,), (1,)), ((), ())),
        precision=lax.Precision.HIGH, preferred_element_type=jnp.float32,
    )


def exchange(pieces, axes):
    return lax.all_to_all(pieces, axes, split_axis=0, concat_axis=0, tiled=True)


def swap(values, axis, mask):
    size = lax.axis_size(axis)
    return lax.ppermute(values, axis, [(k, k ^ mask) for k in range(size)])


def to_all(held, axes, size):
    return exchange(jnp.broadcast_to(held, (size,) + held.shape), axes)


def per_device(
    up_inputs,
    up_grads,
    down_inputs,
    down_grads,
    up_in_proj,
    up_out_proj,
    down_in_proj,
    down_out_proj,
    queries,
):
    zls, xs, cores, ys, zhs = SIZES
    rank = up_in_proj.shape[1]
    rows = 2 * rank // ys // zhs
    other = swap(queries, "zh", 1)
    wide_proj = lax.optimization_barrier(jnp.concatenate([up_out_proj, down_in_proj], axis=1))
    up_in = project_columns(up_inputs, up_in_proj)
    up_out = project_columns(up_grads, wide_proj[:, :rank])
    down_in = project_columns(down_inputs, wide_proj[:, rank:])
    down_out = project_columns(down_grads, down_out_proj)
    pieces = []
    for outs, ins in ((up_out, up_in), (down_out, down_in)):
        for k in range(rank // (zhs * rows)):
            pieces.append(jnp.concatenate([outs[k * zhs * rows : (k + 1) * zhs * rows], ins], axis=0))
    pieces = jnp.stack(pieces)
    y = lax.axis_index("y")
    piece = lambda k: lax.dynamic_index_in_dim(pieces, k, 0, keepdims=False)
    outer = zhs * rows
    half = piece(y) + sum(
        from_sent(swap(to_send(piece(y ^ mask), outer), "y", mask), outer) for mask in (1, 2, 3)
    )
    sums = half + swap(half, "zh", 1)
    outs, ins = sums[:outer], sums[outer:]
    own = outer_rows(jnp.concatenate([outs[0::2], outs[1::2]], axis=0), ins)
    own = jnp.concatenate([own[:rows], own[rows:]], axis=1)
    every = to_all(own.astype(jnp.bfloat16), DP, zls * xs * cores)
    first_half = lax.axis_index("zh") == 0
    low, high = jnp.where(first_half, queries, other), jnp.where(first_half, other, queries)
    scores = lax.dot_general(
        every.reshape(every.shape[0], -1), jnp.concatenate([low, high], axis=1), (((1,), (1,)), ((), ())),
        preferred_element_type=jnp.float32,
    )
    from_1, from_2, from_3 = (swap(scores, "y", mask) for mask in (1, 2, 3))
    return (from_2 + from_3) + (from_1 + scores)


def solution(mesh):
    split = Mesh(mesh.devices.reshape(SIZES), NAMES)
    placed = (
        P(DP, None, TENSOR),
        P(DP, None, TENSOR),
        P(DP, None, TENSOR),
        P(DP, None, TENSOR),
        P(TENSOR, None),
        P(TENSOR, None),
        P(TENSOR, None),
        P(TENSOR, None),
        P(DP, TENSOR),
    )
    return jax.shard_map(
        per_device, mesh=split, in_specs=placed, out_specs=P(None, DP), check_vma=False
    )
```

```python
import jax
import jax.numpy as jnp
from jax import lax
from jax.sharding import Mesh, PartitionSpec as P

SIZES = (4, 4, 2, 4, 2)
NAMES = ("zl", "x", "c", "y", "zh")
DP = ("zl", "x", "c")
TENSOR = ("y", "zh")


def project_columns(acts, proj):
    return lax.dot_general(
        proj, acts[0], (((0,), (1,)), ((), ())), preferred_element_type=jnp.float32
    )


def to_send(sums, outer):
    high = lax.reduce_precision(sums[:outer], 8, 7)
    return jnp.concatenate([high, sums[:outer] - high, sums[outer:]], axis=0).astype(jnp.bfloat16)


def from_sent(sent, outer):
    sums = sent.astype(jnp.float32)
    return jnp.concatenate([sums[:outer] + sums[outer : 2 * outer], sums[2 * outer :]], axis=0)


def outer_rows(outs, ins):
    return lax.dot_general(
        outs, ins, (((1,), (1,)), ((), ())),
        precision=lax.Precision.HIGHEST, preferred_element_type=jnp.float32,
    )


def exchange(pieces, axes):
    return lax.all_to_all(pieces, axes, split_axis=0, concat_axis=0, tiled=True)


def swap(values, axis, mask):
    size = lax.axis_size(axis)
    return lax.ppermute(values, axis, [(k, k ^ mask) for k in range(size)])


def to_all(held, axes, size):
    return exchange(jnp.broadcast_to(held, (size,) + held.shape), axes)


def per_device(
    up_inputs,
    up_grads,
    down_inputs,
    down_grads,
    up_in_proj,
    up_out_proj,
    down_in_proj,
    down_out_proj,
    queries,
):
    zls, xs, cores, ys, zhs = SIZES
    rank = up_in_proj.shape[1]
    rows = 2 * rank // ys // zhs
    other = swap(queries, "zh", 1)
    wide_proj = lax.optimization_barrier(jnp.concatenate([up_out_proj, down_in_proj], axis=1))
    up_in = project_columns(up_inputs, up_in_proj)
    up_out = project_columns(up_grads, wide_proj[:, :rank])
    down_in = project_columns(down_inputs, wide_proj[:, rank:])
    down_out = project_columns(down_grads, down_out_proj)
    pieces = []
    for outs, ins in ((up_out, up_in), (down_out, down_in)):
        for k in range(rank // (zhs * rows)):
            pieces.append(jnp.concatenate([outs[k * zhs * rows : (k + 1) * zhs * rows], ins], axis=0))
    y = lax.axis_index("y")
    pick = lambda table, k: lax.dynamic_index_in_dim(table, k, 0, keepdims=False)
    outer = zhs * rows
    sent = jnp.stack([to_send(piece, outer) for piece in pieces])
    half = pick(jnp.stack(pieces), y) + sum(
        from_sent(swap(pick(sent, y ^ mask), "y", mask), outer) for mask in (1, 3, 2)
    )
    sums = half + swap(half, "zh", 1)
    outs, ins = sums[:outer], sums[outer:]
    own = outer_rows(jnp.concatenate([outs[0::2], outs[1::2]], axis=0), ins)
    own = jnp.concatenate([own[:rows], own[rows:]], axis=1)
    every = to_all(own.astype(jnp.bfloat16), DP, zls * xs * cores)
    first_half = lax.axis_index("zh") == 0
    low, high = jnp.where(first_half, queries, other), jnp.where(first_half, other, queries)
    scores = lax.dot_general(
        every.reshape(every.shape[0], -1), jnp.concatenate([low, high], axis=1), (((1,), (1,)), ((), ())),
        preferred_element_type=jnp.float32,
    )
    from_1, from_2, from_3 = (swap(scores, "y", mask) for mask in (1, 2, 3))
    return (from_2 + from_3) + (from_1 + scores)


def solution(mesh):
    split = Mesh(mesh.devices.reshape(SIZES), NAMES)
    placed = (
        P(DP, None, TENSOR),
        P(DP, None, TENSOR),
        P(DP, None, TENSOR),
        P(DP, None, TENSOR),
        P(TENSOR, None),
        P(TENSOR, None),
        P(TENSOR, None),
        P(TENSOR, None),
        P(DP, TENSOR),
    )
    return jax.shard_map(
        per_device, mesh=split, in_specs=placed, out_specs=P(None, DP), check_vma=False
    )
```
